512 devices in a mesh: dp: 16 (over y, z_hi), tensor: 32 (over z_lo, x, core).
Axes of the slice: x: 4, y: 4, z: 16 (z_hi: 4, z_lo: 4; z = z_hi * 4 + z_lo), core: 2. Of those that a mesh axis runs over, the one named last changes fastest.
Arguments:
- tokens: bfloat16 [65536, 6144], P(('dp', 'tensor')), may hold values from -6 to 6
- expert_ids: int32 [65536, 2], P(('dp', 'tensor')), may hold values from 0 to 7, as said below
- slots: int32 [65536, 2], P(('dp', 'tensor')), may hold values from 0 to 128, as said below
- route_gates: float32 [65536, 2], P(('dp', 'tensor')), may hold values from 0.2 to 1
- w_gate: bfloat16 [6144, 16384], P('dp', 'tensor'), may hold values from -0.078125 to 0.078125
- w_up: bfloat16 [6144, 16384], P('dp', 'tensor'), may hold values from -0.078125 to 0.078125
- w_down: bfloat16 [16384, 6144], P('tensor', 'dp'), may hold values from -0.046875 to 0.046875
Outputs:
- mixed: bfloat16 [65536, 6144], P(('dp', 'tensor'))
The draws below stay inside these ranges and needn't reach their ends.
Inputs may be any that keep to these rules, and one draw needn't show every extreme that they name: `expert_ids`: each token names 2 different experts; every expert is named somewhere. Each device holds 128 consecutive tokens. A route's slot is (the device's index along tensor) * 4 plus the number of earlier routes of the same device to the same expert (tokens in order, then a token's routes in order) when that number is under 4, else 128 (dropped). In every draw all 128 slots of expert 0 of some group are used and some routes are dropped.
All inputs are finite; a program needn't handle non-finite values.
Results may differ from the reference program's by a relative error of at most 0.005.
Values may be sent and summed in bfloat16 or wider, within the bound.
No kernel may reach another device: no remote copies, remote signals or barrier semaphores. Data moves between devices by JAX's collectives and lax.ppermute only.
A program may use at most 64 MiB of HBM per device.

```python
import jax
import jax.numpy as jnp
from jax import lax

D = 6144
FF = 16384
EXPERTS = 8
TOP = 2
SLOT_DEV = 4
TOK_DEV = 128
TOKENS = 65536
N_DP = 16
N_TENSOR = 32


def route_table(key):
    devices = N_DP * N_TENSOR
    key_count, key_group, key_order, key_choice, key_first, key_second = jax.random.split(key, 6)
    counts = jax.random.randint(key_count, (devices,), SLOT_DEV // 2, 2 * SLOT_DEV + 1)
    full_group = jax.random.randint(key_group, (), 0, N_DP)
    owners = jnp.arange(devices, dtype=jnp.int32) // N_TENSOR
    counts = jnp.where(owners == full_group, jnp.maximum(counts, SLOT_DEV + 1), counts)
    scores = jax.random.randint(key_order, (devices, TOK_DEV), 0, 1 << 20) * TOK_DEV + jnp.arange(TOK_DEV, dtype=jnp.int32)
    orders = jnp.argsort(jnp.argsort(scores, axis=1), axis=1)
    chosen = orders < counts[:, None]
    which = jax.random.randint(key_choice, (devices, TOK_DEV), 0, 2)
    first = jax.random.randint(key_first, (devices, TOK_DEV), 1, EXPERTS)
    second = 1 + (first - 1 + jax.random.randint(key_second, (devices, TOK_DEV), 1, EXPERTS - 1)) % (EXPERTS - 1)
    left = jnp.where(chosen & (which == 0), 0, first)
    right = jnp.where(chosen, jnp.where(which == 0, first, 0), second)
    table = jnp.stack([left, right], axis=-1).astype(jnp.int32)
    flat = table.reshape(devices, TOK_DEV * TOP)
    matches = (flat[:, :, None] == jnp.arange(EXPERTS, dtype=jnp.int32)).astype(jnp.int32)
    earlier = jnp.cumsum(matches, axis=1) - matches
    place = jnp.sum(earlier * matches, axis=2)
    offsets = jnp.arange(devices, dtype=jnp.int32) % N_TENSOR * SLOT_DEV
    placed = jnp.where(place < SLOT_DEV, offsets[:, None] + place, SLOT_DEV * N_TENSOR)
    return (table.reshape(devices * TOK_DEV, TOP), placed.reshape(devices * TOK_DEV, TOP).astype(jnp.int32))


def draw_expert_ids(key, part):
    shared = route_table(key)
    return shared[0]


def draw_slots(key, part):
    shared = route_table(key)
    return shared[1]


def block_levels(stream_key, dims, pieces, low, largest):
    def one(axis_at, blocks):
        steps = jax.random.uniform(jax.random.fold_in(jax.random.fold_in(stream_key, 6), axis_at), (blocks,), jnp.float32, low / len(pieces), largest / len(pieces))
        return jnp.repeat(jnp.exp(steps), dims[axis_at] // blocks).reshape((-1,) + (1,) * (len(dims) - axis_at - 1))

    gain = one(*pieces[0])
    for cut in pieces[1:]:
        gain = gain * one(*cut)
    return gain


def normal_values(own_key, shape, spread, reach, shards=(), kind=jnp.bfloat16):
    result = jax.random.normal(own_key, shape, jnp.float32) * spread
    if len(shards) > 0:
        result = block_levels(own_key, shape, shards, -0.22, 0.18) * result
    return jnp.clip(result, min=-reach, max=reach).astype(kind)


def setup_inputs(seed: int = 0) -> dict:
    key_list = jax.random.split(jax.random.key(seed), 8)
    tokens = normal_values(key_list[0], (TOKENS, D), 1.0, 6.0, ((0, 512),))
    expert_ids = draw_expert_ids(jax.random.fold_in(key_list[7], 71), 0)
    slots = draw_slots(jax.random.fold_in(key_list[7], 71), 0)
    route_gates = jnp.clip(0.2 + 0.8 * jax.random.uniform(key_list[3], (TOKENS, TOP), jnp.float32) ** block_levels(key_list[3], (TOKENS, TOP), ((0, 512),), -0.2, 0.2), 0.2, 1.0)
    w_gate = normal_values(key_list[4], (D, FF), D ** -0.5, 0.078125, ((0, 16), (1, 32)))
    w_up = normal_values(key_list[5], (D, FF), D ** -0.5, 0.078125, ((0, 16), (1, 32)))
    w_down = normal_values(key_list[6], (FF, D), FF ** -0.5, 0.046875, ((0, 32), (1, 16)))
    return {"tokens": tokens, "expert_ids": expert_ids, "slots": slots, "route_gates": route_gates, "w_gate": w_gate, "w_up": w_up, "w_down": w_down}


def reference(tokens, expert_ids, slots, route_gates, w_gate, w_up, w_down):
    capacity = SLOT_DEV * N_TENSOR
    group_rows = TOK_DEV * N_TENSOR
    positions = jnp.arange(capacity, dtype=jnp.int32)

    def one_group(group_index):
        first_row = (group_index * group_rows).astype(jnp.int32)
        token_rows = lax.dynamic_slice_in_dim(tokens, first_row, group_rows, 0)
        group_ids = lax.dynamic_slice_in_dim(expert_ids, first_row, group_rows, 0)
        group_slots = lax.dynamic_slice_in_dim(slots, first_row, group_rows, 0)
        group_gates = lax.dynamic_slice_in_dim(route_gates, first_row, group_rows, 0)
        target = jnp.where(group_ids == 0, group_slots, capacity)
        route_hits = (target[:, :, None] == positions).astype(jnp.float32)
        placing = jnp.sum(route_hits, axis=1).astype(jnp.bfloat16)
        slot_block = jnp.dot(placing.T, token_rows, preferred_element_type=jnp.float32).astype(jnp.bfloat16)
        gate_sum = jnp.dot(slot_block, w_gate, preferred_element_type=jnp.float32)
        up_sum = jnp.dot(slot_block, w_up, preferred_element_type=jnp.float32)
        hidden = (jax.nn.silu(gate_sum) * up_sum).astype(jnp.bfloat16)
        expert_out = jnp.dot(hidden, w_down, preferred_element_type=jnp.float32)
        mixing = jnp.sum(route_hits * group_gates[:, :, None], axis=1)
        combined = jnp.dot(mixing, expert_out, precision=lax.Precision.HIGHEST,
                           preferred_element_type=jnp.float32)
        return combined.astype(jnp.bfloat16)

    outputs = lax.map(one_group, jnp.arange(N_DP, dtype=jnp.int32))
    return outputs.reshape(N_DP * group_rows, D)
```

```python
import jax
import jax.numpy as jnp
from jax import lax
from jax.sharding import Mesh
from jax.sharding import PartitionSpec as P

SLOT_DEV = 4
AXES = ("y", "zh", "zl", "x", "c")
SIZES = (4, 4, 4, 4, 2)
CHUNKS = 1
XC = False
BF16, F32 = jnp.bfloat16, jnp.float32


def exchange(pieces, axis):
    return lax.all_to_all(pieces, axis, 0, 0, tiled=True)


def spread(block, axis, size):
    return exchange(jnp.broadcast_to(block[None], (size, *block.shape)), axis)


def per_device(tokens, expert_ids, slots, route_gates, w_gate, w_up, w_down):
    ny, ns, nl, nx, nc = SIZES
    d = tokens.shape[1]
    piece = d // (ny * ns)
    cols = ny * piece
    ff = w_gate.shape[1]
    part = ff // CHUNKS
    swap = [(0, 1), (1, 0)]

    stacked = []
    for k in range(CHUNKS):
        stacked += [w_gate[:, k * part : (k + 1) * part], w_up[:, k * part : (k + 1) * part]]
    in_rows = lax.all_gather(jnp.concatenate(stacked, axis=1), "y", axis=0, tiled=True)
    down_cols = lax.all_gather(w_down, "y", axis=1, tiled=True)

    slot_base = lax.axis_index(("zl", "x", "c")) * SLOT_DEV
    local_slot = jnp.where(expert_ids == 0, slots - slot_base, SLOT_DEV)
    positions = jnp.arange(SLOT_DEV, dtype=jnp.int32)
    route_hits = (local_slot[:, :, None] == positions).astype(F32)
    placing = jnp.sum(route_hits, axis=1).astype(BF16)
    mixing = jnp.sum(route_hits * route_gates[:, :, None], axis=1)
    sending = lax.dot_general(
        placing, tokens, (((0,), (0,)), ((), ())), preferred_element_type=F32
    ).astype(BF16)

    with jax.named_scope("spread_rows"):
        parts = jnp.transpose(sending.reshape(SLOT_DEV, ny, ns, piece), (2, 0, 1, 3))
        parts = parts.reshape(ns, 1, SLOT_DEV, cols)
        parts = jnp.broadcast_to(parts, (ns, nl, SLOT_DEV, cols)).reshape(ns * nl, SLOT_DEV, cols)
        rows = exchange(parts, ("zh", "zl")).reshape(ns * nl * SLOT_DEV, cols)
        rows = spread(rows, "x", nx)
        few = nl * SLOT_DEV
        rows = jnp.transpose(rows.reshape(nx, ns, few, cols), (1, 0, 2, 3))
        rows = rows.reshape(ns, nx * few, cols)
        other = lax.ppermute(rows, "c", swap)
        block = jnp.concatenate([rows, other], axis=1)
        many = nc * nx * few
        block = block.reshape(ns * many, cols)

    with jax.named_scope("expert"):
        sums = []
        for k in range(CHUNKS):
            both = jnp.dot(
                block, in_rows[:, 2 * part * k : 2 * part * (k + 1)], preferred_element_type=F32
            ).astype(BF16)
            sums.append(exchange(both.reshape(ns, many, 2 * part), "zh"))
        total = None
        for k in range(CHUNKS):
            both = jnp.sum(sums[k].astype(F32), axis=0)
            hidden = (jax.nn.silu(both[:, :part]) * both[:, part:]).astype(BF16)
            hidden = spread(hidden, "zh", ns)
            if XC:
                hidden = jnp.transpose(hidden.reshape(ns, nc, nx, few, part), (2, 1, 0, 3, 4))
            else:
                hidden = jnp.transpose(hidden.reshape(ns, nc, nx, few, part), (1, 2, 0, 3, 4))
            hidden = hidden.reshape(ns * many, part)
            terms = jnp.dot(
                hidden, down_cols[part * k : part * (k + 1)], preferred_element_type=F32
            )
            total = terms if total is None else total + terms

    with jax.named_scope("collect"):
        if XC:
            mine = lax.axis_index("c")
            terms = total.reshape(nx, 2, ns * few, cols)
            terms = jnp.where(mine == 0, terms, terms[:, ::-1])
            terms = terms.astype(BF16).reshape(nx * 2, ns * few, cols)
            terms = exchange(terms, ("x", "c"))
        else:
            terms = total.reshape(nc, nx * ns * few, cols)
            terms = terms[0] + lax.ppermute(terms[1], "c", swap)
            terms = exchange(terms.astype(BF16).reshape(nx, ns * few, cols), "x")
        terms = jnp.sum(terms.astype(F32), axis=0)
        terms = exchange(terms.reshape(ns * nl, SLOT_DEV, cols), ("zh", "zl"))
        terms = jnp.sum(terms.reshape(ns, nl, SLOT_DEV, cols), axis=1)

    with jax.named_scope("mix"):
        terms = jnp.transpose(terms.reshape(ns, SLOT_DEV, ny, piece), (1, 2, 0, 3))
        expert_out = terms.reshape(SLOT_DEV, d)
        out = mixing[:, 0:1] * expert_out[0:1]
        for s in range(1, SLOT_DEV):
            out = out + mixing[:, s : s + 1] * expert_out[s : s + 1]
    return out.astype(BF16)


def solution(mesh):
    fine = Mesh(mesh.devices.reshape(SIZES), AXES)
    rows = P(AXES, None)
    dp, tensor = AXES[:2], AXES[2:]
    return jax.shard_map(
        per_device,
        mesh=fine,
        in_specs=(rows, rows, rows, rows, P(dp, tensor), P(dp, tensor), P(tensor, dp)),
        out_specs=rows,
        check_vma=False,
    )
```

```python
import jax
import jax.numpy as jnp
from jax import lax
from jax.sharding import Mesh
from jax.sharding import PartitionSpec as P

SLOT_DEV = 4
AXES = ("y", "zh", "zl", "x", "c")
SIZES = (4, 4, 4, 4, 2)
CHUNKS = 2
AG = "pp"
XC = False
BF16, F32 = jnp.bfloat16, jnp.float32


def exchange(pieces, axis):
    return lax.all_to_all(pieces, axis, 0, 0, tiled=True)


def spread(block, axis, size):
    return exchange(jnp.broadcast_to(block[None], (size, *block.shape)), axis)


def send(block, axis, size, steps):
    return lax.ppermute(block, axis, [(i, (i + steps) % size) for i in range(size)])


def per_device(tokens, expert_ids, slots, route_gates, w_gate, w_up, w_down):
    ny, ns, nl, nx, nc = SIZES
    d = tokens.shape[1]
    piece = d // (ny * ns)
    cols = ny * piece
    ff = w_gate.shape[1]
    part = ff // CHUNKS
    swap = [(0, 1), (1, 0)]

    stacked = []
    for k in range(CHUNKS):
        stacked += [w_gate[:, k * part : (k + 1) * part], w_up[:, k * part : (k + 1) * part]]
    in_rows = [
        lax.all_gather(jnp.concatenate(stacked[2 * k : 2 * k + 2], axis=1), "y", axis=0, tiled=True)
        for k in range(CHUNKS)
    ]
    down_cols = lax.all_gather(w_down, "y", axis=1, tiled=True)

    slot_base = lax.axis_index(("zl", "x", "c")) * SLOT_DEV
    local_slot = jnp.where(expert_ids == 0, slots - slot_base, SLOT_DEV)
    positions = jnp.arange(SLOT_DEV, dtype=jnp.int32)
    route_hits = (local_slot[:, :, None] == positions).astype(F32)
    placing = jnp.sum(route_hits, axis=1).astype(BF16)
    mixing = jnp.sum(route_hits * route_gates[:, :, None], axis=1)
    sending = lax.dot_general(
        placing, tokens, (((0,), (0,)), ((), ())), preferred_element_type=F32
    ).astype(BF16)

    with jax.named_scope("spread_rows"):
        parts = jnp.transpose(sending.reshape(SLOT_DEV, ny, ns, piece), (2, 0, 1, 3))
        parts = parts.reshape(ns, 1, SLOT_DEV, cols)
        parts = jnp.broadcast_to(parts, (ns, nl, SLOT_DEV, cols)).reshape(ns * nl, SLOT_DEV, cols)
        rows = exchange(parts, ("zh", "zl")).reshape(ns * nl * SLOT_DEV, cols)
        rows = spread(rows, "x", nx)
        few = nl * SLOT_DEV
        rows = jnp.transpose(rows.reshape(nx, ns, few, cols), (1, 0, 2, 3))
        rows = rows.reshape(ns, nx * few, cols)
        other = lax.ppermute(rows, "c", swap)
        block = jnp.concatenate([rows, other], axis=1)
        many = nc * nx * few
        block = block.reshape(ns * many, cols)

    with jax.named_scope("expert"):
        zh = lax.axis_index("zh")
        block = block.reshape(ns, many, cols)

        order = sorted(range(1, ns), key=lambda k: -min(k, ns - k))
        gathered = []
        for h in range(CHUNKS):

            def product(k):
                picked = lax.dynamic_index_in_dim(block, (zh + k) % ns, 0, keepdims=False)
                return jnp.dot(picked, in_rows[h], preferred_element_type=F32)

            arrived = [send(product(k).astype(BF16), "zh", ns, k) for k in order]
            both = product(0)
            for term in arrived:
                both = both + term.astype(F32)
            hidden = (jax.nn.silu(both[:, :part]) * both[:, part:]).astype(BF16)
            if AG == "pp":
                got = {k: send(hidden, "zh", ns, -k) for k in order}
                got[0] = hidden
                gathered.append(jnp.stack([got[k] for k in range(ns)]))
            else:
                gathered.append(hidden)
        hidden = jnp.concatenate(gathered, axis=-1)
        if AG != "pp":
            hidden = spread(hidden, "zh", ns)
        hidden = jnp.transpose(hidden.reshape(ns, nc, nx, few, ff), (1, 2, 0, 3, 4))
        total = jnp.dot(hidden.reshape(ns * many, ff), down_cols, preferred_element_type=F32)

    with jax.named_scope("collect"):
        if XC:
            mine = lax.axis_index("c")
            terms = total.reshape(nx, 2, ns * few, cols)
            terms = jnp.where(mine == 0, terms, terms[:, ::-1])
            terms = terms.astype(BF16).reshape(nx * 2, ns * few, cols)
            terms = exchange(terms, ("x", "c"))
        else:
            terms = total.reshape(nc, nx * ns * few, cols)
            terms = terms[0] + lax.ppermute(terms[1], "c", swap)
            terms = exchange(terms.astype(BF16).reshape(nx, ns * few, cols), "x")
        terms = jnp.sum(terms.astype(F32), axis=0)
        terms = terms.reshape(ns, nl, SLOT_DEV, cols)
        terms = jnp.concatenate([terms, terms[:-1]], axis=0)
        terms = lax.dynamic_slice_in_dim(terms, (ns - zh) % ns, ns, 0)
        terms = terms.astype(BF16).reshape(ns * nl, SLOT_DEV, cols)
        terms = exchange(terms, ("zh", "zl")).astype(F32)
        terms = jnp.sum(terms.reshape(ns, nl, SLOT_DEV, cols), axis=1)

    with jax.named_scope("mix"):
        terms = jnp.transpose(terms.reshape(ns, SLOT_DEV, ny, piece), (1, 2, 0, 3))
        expert_out = terms.reshape(SLOT_DEV, d)
        out = mixing[:, 0:1] * expert_out[0:1]
        for s in range(1, SLOT_DEV):
            out = out + mixing[:, s : s + 1] * expert_out[s : s + 1]
    return out.astype(BF16)


def solution(mesh):
    fine = Mesh(mesh.devices.reshape(SIZES), AXES)
    rows = P(AXES, None)
    dp, tensor = AXES[:2], AXES[2:]
    return jax.shard_map(
        per_device,
        mesh=fine,
        in_specs=(rows, rows, rows, rows, P(dp, tensor), P(dp, tensor), P(tensor, dp)),
        out_specs=rows,
        check_vma=False,
    )
```

```python
import jax
import jax.numpy as jnp
from jax import lax
from jax.sharding import Mesh
from jax.sharding import PartitionSpec as P

SLOT_DEV = 4
AXES = ("y", "zh", "zl", "x", "c")
SIZES = (4, 4, 4, 4, 2)
PARTS = (512,)
SUMS, SPREADS = ("pp",), ("a2a",)
BF16, F32 = jnp.bfloat16, jnp.float32


def exchange(pieces, axis):
    return lax.all_to_all(pieces, axis, 0, 0, tiled=True)


def spread(block, axis, size):
    return exchange(jnp.broadcast_to(block[None], (size, *block.shape)), axis)


def send(block, axis, size, steps):
    return lax.ppermute(block, axis, [(i, (i + steps) % size) for i in range(size)])


def per_device(tokens, expert_ids, slots, route_gates, w_gate, w_up, w_down):
    ny, ns, nl, nx, nc = SIZES
    d = tokens.shape[1]
    piece = d // (ny * ns)
    cols = ny * piece
    ff = w_gate.shape[1]
    swap = [(0, 1), (1, 0)]

    in_rows, at = [], 0
    for part in PARTS:
        own = jnp.concatenate([w_gate[:, at : at + part], w_up[:, at : at + part]], axis=1)
        in_rows.append(lax.all_gather(own, "y", axis=0, tiled=True))
        at += part
    down_cols = lax.all_gather(w_down, "y", axis=1, tiled=True)

    slot_base = lax.axis_index(("zl", "x", "c")) * SLOT_DEV
    local_slot = jnp.where(expert_ids == 0, slots - slot_base, SLOT_DEV)
    positions = jnp.arange(SLOT_DEV, dtype=jnp.int32)
    route_hits = (local_slot[:, :, None] == positions).astype(F32)
    placing = jnp.sum(route_hits, axis=1).astype(BF16)
    mixing = jnp.sum(route_hits * route_gates[:, :, None], axis=1)
    sending = lax.dot_general(
        placing, tokens, (((0,), (0,)), ((), ())), preferred_element_type=F32
    ).astype(BF16)

    with jax.named_scope("spread_rows"):
        parts = jnp.transpose(sending.reshape(SLOT_DEV, ny, ns, piece), (2, 0, 1, 3))
        parts = parts.reshape(ns, 1, SLOT_DEV, cols)
        parts = jnp.broadcast_to(parts, (ns, nl, SLOT_DEV, cols)).reshape(ns * nl, SLOT_DEV, cols)
        rows = exchange(parts, ("zh", "zl")).reshape(ns * nl * SLOT_DEV, cols)
        rows = spread(rows, "x", nx)
        few = nl * SLOT_DEV
        rows = jnp.transpose(rows.reshape(nx, ns, few, cols), (1, 0, 2, 3))
        rows = rows.reshape(ns, nx * few, cols)
        other = lax.ppermute(rows, "c", swap)
        block = jnp.concatenate([rows, other], axis=1)
        many = nc * nx * few
        block = block.reshape(ns * many, cols)

    with jax.named_scope("expert"):
        zh = lax.axis_index("zh")
        block = block.reshape(ns, many, cols)

        order = sorted(range(1, ns), key=lambda k: -min(k, ns - k))
        gathered = []
        for h, part in enumerate(PARTS):

            def product(k):
                picked = lax.dynamic_index_in_dim(block, (zh + k) % ns, 0, keepdims=False)
                return jnp.dot(picked, in_rows[h], preferred_element_type=F32)

            if SUMS[h] == "pp":
                far = product(2).astype(BF16)
                mid = many // 2
                above = send(far[:mid], "zh", ns, 1).astype(F32)
                below = send(far[mid:], "zh", ns, -1).astype(F32)
                ahead, back = product(1), product(ns - 1)
                ahead = jnp.concatenate([ahead[:mid] + above, ahead[mid:]], axis=0)
                back = jnp.concatenate([back[:mid], back[mid:] + below], axis=0)
                ahead = send(ahead.astype(BF16), "zh", ns, 1)
                back = send(back.astype(BF16), "zh", ns, -1)
                both = product(0) + ahead.astype(F32) + back.astype(F32)
            else:
                both = jnp.dot(
                    block.reshape(ns * many, cols), in_rows[h], preferred_element_type=F32
                )
                both = exchange(both.astype(BF16).reshape(ns, many, 2 * part), "zh")
                both = jnp.sum(both.astype(F32), axis=0)
            hidden = (jax.nn.silu(both[:, :part]) * both[:, part:]).astype(BF16)
            if SPREADS[h] == "pp":
                got = {k: send(hidden, "zh", ns, -k) for k in order}
                got[0] = hidden
                turned = jnp.stack([got[k] for k in [*range(ns), *range(ns - 1)]])
                gathered.append(lax.dynamic_slice_in_dim(turned, (ns - zh) % ns, ns, 0))
            else:
                gathered.append(spread(hidden, "zh", ns))
        hidden = jnp.concatenate(gathered, axis=-1)
        hidden = jnp.transpose(hidden.reshape(ns, nc, nx, few, ff), (1, 2, 0, 3, 4))
        total = jnp.dot(hidden.reshape(ns * many, ff), down_cols, preferred_element_type=F32)

    with jax.named_scope("collect"):
        terms = total.reshape(nc, nx * ns * few, cols)
        terms = terms[0] + lax.ppermute(terms[1], "c", swap)
        terms = exchange(terms.astype(BF16).reshape(nx, ns * few, cols), "x")
        terms = jnp.sum(terms.astype(F32), axis=0)
        terms = terms.reshape(ns, nl, SLOT_DEV, cols)
        terms = terms.astype(BF16).reshape(ns * nl, SLOT_DEV, cols)
        terms = exchange(terms, ("zh", "zl")).astype(F32)
        terms = jnp.sum(terms.reshape(ns, nl, SLOT_DEV, cols), axis=1)

    with jax.named_scope("mix"):
        terms = jnp.transpose(terms.reshape(ns, SLOT_DEV, ny, piece), (1, 2, 0, 3))
        expert_out = terms.reshape(SLOT_DEV, d)
        out = mixing[:, 0:1] * expert_out[0:1]
        for s in range(1, SLOT_DEV):
            out = out + mixing[:, s : s + 1] * expert_out[s : s + 1]
    return out.astype(BF16)


def solution(mesh):
    fine = Mesh(mesh.devices.reshape(SIZES), AXES)
    rows = P(AXES, None)
    dp, tensor = AXES[:2], AXES[2:]
    return jax.shard_map(
        per_device,
        mesh=fine,
        in_specs=(rows, rows, rows, rows, P(dp, tensor), P(dp, tensor), P(tensor, dp)),
        out_specs=rows,
        check_vma=False,
    )
```
